256 devices in a mesh: batch: 32 (over x, y, core), tensor: 8 (over z).
Axes of the slice: x: 4, y: 4, z: 8, core: 2. Of those that a mesh axis runs over, the one named last changes fastest.
Arguments:
- tokens: bfloat16 [4, 128, 8192], P(None, None, 'batch'), may hold values from -96 to 96, as said below
- attn_gain: bfloat16 [8192], P('batch'), may hold values from 0.099609375 to 1.8984375
- w_query: bfloat16 [8192, 8192], P('batch', 'tensor'), may hold values from -0.0625 to 0.0625
- query_gain: bfloat16 [128], replicated, may hold values from 0.099609375 to 1.8984375
- keys: bfloat16 [32, 8, 6400, 128], P('batch', 'tensor'), may hold values from -260 to 260
- values: bfloat16 [32, 8, 6400, 128], P('batch', 'tensor'), may hold values from -18 to 18
- w_out: bfloat16 [8192, 8192], P('tensor', 'batch'), may hold values from -0.0625 to 0.0625
- ffn_gain: bfloat16 [8192], P('batch'), may hold values from 0.099609375 to 1.8984375
- w_gate: bfloat16 [8192, 28672], P('batch', 'tensor'), may hold values from -0.0625 to 0.0625
- w_up: bfloat16 [8192, 28672], P('batch', 'tensor'), may hold values from -0.0625 to 0.0625
- w_down: bfloat16 [28672, 8192], P('tensor', 'batch'), may hold values from -0.03125 to 0.03125
- citers: int32 [32, 15], P('batch'), may hold values from -1 to 127, as said below
- cite_owner: int32 [128, 2], P('batch'), may hold values from 0 to 31, as said below
- cite_slot: int32 [128, 2], P('batch'), may hold values from 0 to 14, as said below
Outputs:
- mixed: bfloat16 [4, 128, 8192], P(None, 'tensor', 'batch')
The draws below stay inside these ranges and needn't reach their ends.
Inputs may be any that keep to these rules, and one draw needn't show every extreme that they name: `tokens`: features have scales that differ from column to column and from row to row. `citers`: row i lists in slots 0 to n - 1 the n distinct requests that cite image i, and -1 in its other slots; every image is cited by 1 to 15 requests, and some image by exactly 15. A request's 2 citations name different images; request r appears in the list of image cite_owner[r, c]. citers[cite_owner[r, c], cite_slot[r, c]] = r.
All inputs are finite; a program needn't handle non-finite values.
Results may differ from the reference program's by a relative error of at most 0.013.
Values may be sent and summed in bfloat16 or wider, within the bound.
No kernel may reach another device: no remote copies, remote signals or barrier semaphores. Data moves between devices by JAX's collectives and lax.ppermute only.
A program may use at most 128 MiB of HBM per device.

```python
import math
import jax
import jax.numpy as jnp
from jax import lax

D = 8192
H = 64
KVH = 8
HD = 128
FF = 28672
STEPS = 4
CITE = 2
REQ_DEV = 4
VT = 6400
REQS = 128
IMAGES = 32
LIST = 15
N_BATCH = 32


def citation_table(key):
    key = jax.random.fold_in(key, 7)
    first, second, third, fourth = jax.random.split(key, 4)
    half = IMAGES // 2
    mean_load = 2 * REQ_DEV
    spread = jax.random.randint(first, (half,), 0, mean_load)
    hottest = jax.random.randint(second, (), 0, half)
    spread = jnp.where(jnp.arange(half) == hottest, mean_load - 1, spread)
    loads = jnp.stack([mean_load + spread, mean_load - spread], axis=1).reshape(IMAGES)
    ends = jnp.cumsum(loads)
    starts = ends - loads
    owner_of_rank = jax.random.permutation(third, IMAGES)
    request_order = jax.random.permutation(fourth, REQS)
    position = jnp.arange(CITE * REQS)
    rank = jnp.sum((position[:, None] >= ends[None, :]).astype(jnp.int32), axis=1)
    slot = position - starts[rank]
    owner = owner_of_rank[rank]
    request = request_order[position % REQS]
    which = position // REQS
    cite_owner = jnp.zeros((REQS, CITE), jnp.int32).at[request, which].set(owner.astype(jnp.int32))
    cite_slot = jnp.zeros((REQS, CITE), jnp.int32).at[request, which].set(slot.astype(jnp.int32))
    citers = jnp.full((IMAGES, LIST), -1, jnp.int32).at[owner, slot].set(request.astype(jnp.int32))
    return (citers, cite_owner, cite_slot)


def draw_citers(key, part):
    shared = citation_table(key)
    return shared[0]


def draw_cite_owner(key, part):
    shared = citation_table(key)
    return shared[1]


def draw_cite_slot(key, part):
    shared = citation_table(key)
    return shared[2]


def draw_tokens(key, part):
    key = jax.random.fold_in(key, 11)
    first, second, third = jax.random.split(key, 3)
    columns = jnp.exp(jax.random.uniform(second, (D,), jnp.float32, math.log(0.25), math.log(2.0)))
    position = jnp.arange(D).astype(jnp.float32) / D
    ramp = 1.0 + position
    base = jax.random.normal(first, (STEPS, REQS, D), jnp.float32)
    rows = jnp.exp(jax.random.uniform(third, (STEPS, REQS, 1), jnp.float32, math.log(0.5), math.log(2.0)))
    return (jnp.clip(base, -4.0, 4.0) * columns * ramp * rows).astype(jnp.bfloat16)


def draw_keys(key, part):
    key = jax.random.fold_in(key, 12)
    first = jax.random.fold_in(key, 0)
    base = 2.5 * jnp.clip(jax.random.normal(first, (IMAGES, KVH, VT, HD), jnp.float32), -6.0, 6.0)
    return base.astype(jnp.bfloat16)


def block_levels(own_key, dims, cuts, smallest, largest):
    loudness, own = 1.0, jax.random.fold_in(own_key, 6)
    for dim, blocks in cuts:
        draws = jnp.exp(jax.random.uniform(jax.random.fold_in(own, dim), (blocks,), jnp.float32, smallest / len(cuts), largest / len(cuts)))
        loudness = loudness * jnp.repeat(draws, dims[dim] // blocks).reshape([-1 if axis == dim else 1 for axis in range(len(dims))])
    return loudness


def gaussian(key, shape, width, reach, cuts=(), held_as=jnp.bfloat16):
    array = jax.random.normal(key, shape, jnp.float32) * width
    if len(cuts) > 0:
        array = block_levels(key, shape, cuts, -0.22, 0.18) * array
    return jnp.clip(array, min=-reach, max=reach).astype(held_as)


def setup_inputs(seed: int = 0) -> dict:
    streams_of = jax.random.split(jax.random.key(seed), 15)
    tokens = draw_tokens(jax.random.fold_in(streams_of[14], 71), 0)
    attn_gain = jnp.clip(1.0 + 0.18 * jax.random.normal(streams_of[1], (D,), jnp.float32), 0.099609375, 1.8984375).astype(jnp.bfloat16)
    w_query = gaussian(streams_of[2], (D, H * HD), D ** -0.5, 0.0625, ((0, 32), (1, 8)))
    query_gain = jnp.clip(1.0 + 0.18 * jax.random.normal(streams_of[3], (HD,), jnp.float32), 0.099609375, 1.8984375).astype(jnp.bfloat16)
    keys = draw_keys(jax.random.fold_in(streams_of[14], 71), 0)
    values = gaussian(streams_of[5], (IMAGES, KVH, VT, HD), 3.0, 18.0, ((0, 32), (1, 8)))
    w_out = gaussian(streams_of[6], (H * HD, D), (H * HD) ** -0.5, 0.0625, ((0, 8), (1, 32)))
    ffn_gain = jnp.clip(1.0 + 0.18 * jax.random.normal(streams_of[7], (D,), jnp.float32), 0.099609375, 1.8984375).astype(jnp.bfloat16)
    w_gate = gaussian(streams_of[8], (D, FF), D ** -0.5, 0.0625, ((0, 32), (1, 8)))
    w_up = gaussian(streams_of[9], (D, FF), D ** -0.5, 0.0625, ((0, 32), (1, 8)))
    w_down = gaussian(streams_of[10], (FF, D), FF ** -0.5, 0.03125, ((0, 8), (1, 32)))
    citers = draw_citers(jax.random.fold_in(streams_of[14], 71), 0)
    cite_owner = draw_cite_owner(jax.random.fold_in(streams_of[14], 71), 0)
    cite_slot = draw_cite_slot(jax.random.fold_in(streams_of[14], 71), 0)
    return dict(tokens=tokens, attn_gain=attn_gain, w_query=w_query, query_gain=query_gain, keys=keys, values=values, w_out=w_out, ffn_gain=ffn_gain, w_gate=w_gate, w_up=w_up, w_down=w_down, citers=citers, cite_owner=cite_owner, cite_slot=cite_slot)


EPS = 1e-05

def settle(array_in):
    return lax.optimization_barrier(array_in)

def rms_scale(values_in, gain):
    power = lax.optimization_barrier(jnp.mean(values_in * values_in, axis=-1, keepdims=True))
    return values_in * lax.rsqrt(power + EPS) * gain.astype(jnp.float32)

def reference(tokens, attn_gain, w_query, query_gain, keys, values, w_out, ffn_gain, w_gate, w_up, w_down, citers, cite_owner, cite_slot):
    group = H // KVH
    rows_x = jnp.transpose(tokens.astype(jnp.float32), (1, 0, 2))
    normed = (rows_x * attn_gain.astype(jnp.float32)).astype(jnp.bfloat16)
    query = jnp.dot(normed.reshape(REQS * STEPS, D), w_query, preferred_element_type=jnp.float32)
    query = query.reshape(REQS, STEPS, H, HD)
    power = lax.optimization_barrier(jnp.mean(query * query, axis=-1, keepdims=True))
    query_unit = settle((query * lax.rsqrt(power + EPS) * query_gain.astype(jnp.float32)).astype(jnp.bfloat16))

    def one_image(item):
        listed, image_keys, image_values = item
        picked = query_unit[jnp.maximum(listed, 0)].astype(jnp.float32).reshape(LIST, STEPS, KVH, group, HD)
        scores = jnp.einsum('lsgqd,gkd->glsqk', picked, image_keys.astype(jnp.float32)) * (1.0 / math.sqrt(HD))
        top = lax.optimization_barrier(jnp.max(scores, axis=-1))
        weights = jnp.exp(scores - top[..., None])
        total = lax.optimization_barrier(jnp.sum(weights, axis=-1))
        weights_low = settle(weights.astype(jnp.bfloat16)).astype(jnp.float32)
        numer = jnp.einsum('glsqk,gkd->lsgqd', weights_low, image_values.astype(jnp.float32))
        total_t = jnp.transpose(total, (1, 2, 0, 3))
        part = (numer / total_t[..., None]).reshape(LIST, STEPS, H * HD).astype(jnp.bfloat16)
        lse = jnp.transpose(top, (1, 2, 0, 3)).reshape(LIST, STEPS, H) + jnp.log(total_t.reshape(LIST, STEPS, H))
        lse_high = settle(lse.astype(jnp.bfloat16))
        lse_low = (lse - lse_high.astype(jnp.float32)).astype(jnp.bfloat16)
        return (part, lse_high, lse_low)
    parts, highs, lows = lax.map(one_image, (citers, keys, values))
    parts, highs, lows = settle((parts, highs, lows))
    chosen = parts[cite_owner, cite_slot].astype(jnp.float32).reshape(REQS, CITE, STEPS, H, HD)
    level = highs[cite_owner, cite_slot].astype(jnp.float32) + lows[cite_owner, cite_slot].astype(jnp.float32)
    peak = lax.optimization_barrier(jnp.max(level, axis=1, keepdims=True))
    share = jnp.exp(level - peak)
    share = share / lax.optimization_barrier(jnp.sum(share, axis=1, keepdims=True))
    attended = lax.optimization_barrier(jnp.sum(share[..., None] * chosen, axis=1)).reshape(REQS * STEPS, H * HD).astype(jnp.bfloat16)
    attn_out = jnp.dot(attended, w_out, preferred_element_type=jnp.float32).reshape(REQS, STEPS, D)
    resid = rows_x + attn_out
    normed_ffn = rms_scale(resid, ffn_gain).astype(jnp.bfloat16).reshape(REQS * STEPS, D)
    block_width = D // N_BATCH
    blocks = jnp.transpose(normed_ffn.reshape(REQS * STEPS, N_BATCH, block_width), (1, 0, 2))
    gate_blocks = w_gate.reshape(N_BATCH, block_width, FF)
    up_blocks = w_up.reshape(N_BATCH, block_width, FF)

    def add_block(carry, item):
        piece, gate_piece, up_piece = item
        gated = settle(jnp.dot(piece, gate_piece, preferred_element_type=jnp.float32).astype(jnp.bfloat16))
        lifted = settle(jnp.dot(piece, up_piece, preferred_element_type=jnp.float32).astype(jnp.bfloat16))
        return ((carry[0] + gated.astype(jnp.float32), carry[1] + lifted.astype(jnp.float32)), None)
    zeros = jnp.zeros((REQS * STEPS, FF), jnp.float32)
    (gate, lifted_sum), _ = lax.scan(add_block, (zeros, zeros), (blocks, gate_blocks, up_blocks))
    hidden = (jax.nn.silu(gate) * lifted_sum).astype(jnp.bfloat16)
    down = jnp.dot(hidden, w_down, preferred_element_type=jnp.float32).reshape(REQS, STEPS, D)
    return jnp.transpose((resid + down).astype(jnp.bfloat16), (1, 0, 2))
```

```python
import math

import jax
import jax.numpy as jnp
from jax import lax
from jax.sharding import Mesh, PartitionSpec as P

EPS = 1e-05
ABSENT = -1e30
BF16, F32 = jnp.bfloat16, jnp.float32
SWAP = [(0, 1), (1, 0)]


def swap(value):
    return lax.ppermute(value, "core", SWAP)


def keep_and_send(value, core, axis):
    half = value.shape[axis] // 2
    mine = lax.dynamic_slice_in_dim(value, core * half, half, axis)
    theirs = lax.dynamic_slice_in_dim(value, (1 - core) * half, half, axis)
    return mine, theirs


def share_columns(weight, core):
    mine, theirs = keep_and_send(weight, core, 1)
    return jnp.concatenate([mine, swap(theirs)], axis=0)


def share_rows(weight, core):
    mine, theirs = keep_and_send(weight, core, 0)
    return mine, swap(theirs)


def exchange(value, axis):
    return lax.all_to_all(value, axis, 0, 0, tiled=True)


def gather(value, axis):
    n = lax.axis_size(axis)
    return exchange(jnp.broadcast_to(value[None], (n, *value.shape)), axis)


def dot(left, right):
    return jnp.dot(left, right, preferred_element_type=F32)


def attend(listed, queries, image_keys, image_values):
    picked = queries[jnp.maximum(listed, 0)]
    slots, steps, heads, head_dim = picked.shape
    rows = picked.reshape(slots * steps * heads, head_dim)
    scores = lax.dot_general(rows, image_keys, (((1,), (1,)), ((), ())), preferred_element_type=F32)
    scores = scores * (1.0 / math.sqrt(head_dim))
    top = jnp.max(scores, axis=-1, keepdims=True)
    weights = jnp.exp(scores - top)
    total = jnp.sum(weights, axis=-1, keepdims=True)
    part = (dot(weights.astype(BF16), image_values) / total).astype(BF16)
    lse = top + jnp.log(total)
    return part.reshape(picked.shape), lse.reshape(slots, steps, heads)


def by_request(listed, part, lse, reqs):
    slots, steps, heads, head_dim = part.shape
    hit = jnp.arange(reqs)[:, None] == listed[None, :]
    dense = dot(hit.astype(BF16), part.reshape(slots, -1)).reshape(reqs, steps, heads, head_dim)
    level = jnp.sum(jnp.where(hit[:, :, None, None], lse[None], 0.0), axis=1)
    level = jnp.where(jnp.any(hit, axis=1)[:, None, None], level, ABSENT)
    return dense, level


def per_device(
    tokens, attn_gain, w_query, query_gain, keys, values, w_out, ffn_gain, w_gate, w_up, w_down, citers
):
    core = lax.axis_index("core")
    n_chip, n_tensor = lax.axis_size("chip"), lax.axis_size("tensor")
    steps, reqs, width = tokens.shape
    rows = reqs * steps
    full_width = width * 2 * n_chip
    head_dim = query_gain.shape[0]
    chip_rows = rows // n_chip

    rows_x = jnp.transpose(tokens, (1, 0, 2)).reshape(rows, width)
    normed = (rows_x.astype(F32) * attn_gain.astype(F32)).astype(BF16)
    normed = jnp.concatenate([normed, swap(normed)], axis=1)
    wq = share_columns(w_query, core)
    other_keys, other_values, other_citers = swap(keys[0, 0]), swap(values[0, 0]), swap(citers)
    wo_own, wo_other = share_rows(w_out, core)
    wg, wu = share_columns(w_gate, core), share_columns(w_up, core)
    wd_own, wd_other = share_rows(w_down, core)
    other_gain = swap(ffn_gain)

    query = dot(normed, wq).astype(BF16)
    query = exchange(query.reshape(n_chip, chip_rows, -1), "chip")
    query = jnp.sum(query.astype(F32), axis=0).reshape(chip_rows, -1, head_dim)
    power = jnp.mean(query * query, axis=-1, keepdims=True)
    query = (query * lax.rsqrt(power + EPS) * query_gain.astype(F32)).astype(BF16)
    heads = query.shape[1]
    queries = gather(query.reshape(chip_rows, -1), "chip").reshape(reqs, steps, heads, head_dim)

    one, level_one = by_request(citers[0], *attend(citers[0], queries, keys[0, 0], values[0, 0]), reqs)
    two, level_two = by_request(
        other_citers[0], *attend(other_citers[0], queries, other_keys, other_values), reqs
    )
    peak = jnp.maximum(level_one, level_two)
    weigh_one, weigh_two = jnp.exp(level_one - peak), jnp.exp(level_two - peak)
    total = weigh_one + weigh_two
    part = one * (weigh_one / total)[..., None] + two * (weigh_two / total)[..., None]
    level = jnp.where(peak > 0.5 * ABSENT, peak + jnp.log(total), ABSENT)
    high = lax.optimization_barrier(level.astype(BF16))
    low = (level - high.astype(F32)).astype(BF16)
    pad = jnp.zeros((rows, 128 - 2 * heads), BF16)
    message = jnp.concatenate(
        [part.astype(BF16).reshape(rows, -1), high.reshape(rows, heads), low.reshape(rows, heads), pad],
        axis=1,
    )
    message = exchange(message.reshape(n_chip, chip_rows, -1), "chip")
    columns = heads * head_dim
    part = message[..., :columns].astype(F32).reshape(n_chip, chip_rows, heads, head_dim)
    level = (
        message[..., columns : columns + heads].astype(F32)
        + message[..., columns + heads : columns + 2 * heads].astype(F32)
    )
    share = jnp.exp(level - jnp.max(level, axis=0, keepdims=True))
    share = share / jnp.sum(share, axis=0, keepdims=True)
    attended = jnp.sum(share[..., None] * part, axis=0).reshape(chip_rows, columns).astype(BF16)
    attended = gather(attended, "chip").reshape(rows, columns)

    part_own = dot(attended, wo_own) + swap(dot(attended, wo_other).astype(BF16)).astype(F32)
    part_own = exchange(part_own.astype(BF16).reshape(n_tensor, rows // n_tensor, width), "tensor")
    own_rows = rows // n_tensor
    resid = lax.dynamic_slice_in_dim(rows_x, lax.axis_index("tensor") * own_rows, own_rows, 0)
    resid = resid.astype(F32) + jnp.sum(part_own.astype(F32), axis=0)

    gain = ffn_gain.astype(F32)
    scaled = gather((resid * gain).astype(BF16), "tensor").reshape(rows, width)
    scaled = jnp.concatenate([scaled, swap(scaled)], axis=1)
    both_gain = jnp.concatenate([ffn_gain, other_gain]).astype(F32)
    plain = scaled.astype(F32) / both_gain
    squares = jnp.sum(plain * plain, axis=-1, keepdims=True)
    sq_high = lax.optimization_barrier(squares.astype(BF16))
    sq_low = (squares - sq_high.astype(F32)).astype(BF16)
    sums = jnp.concatenate(
        [dot(scaled, wg).astype(BF16), dot(scaled, wu).astype(BF16), sq_high, sq_low, jnp.zeros((rows, 126), BF16)],
        axis=1,
    )
    sums = exchange(sums.reshape(n_chip, chip_rows, -1), "chip")
    sums = jnp.sum(sums.astype(F32), axis=0)
    units = wg.shape[1]
    squares = sums[:, 2 * units : 2 * units + 1] + sums[:, 2 * units + 1 : 2 * units + 2]
    scale = lax.rsqrt(squares / full_width + EPS)
    gate, up = sums[:, :units] * scale, sums[:, units : 2 * units] * scale
    hidden = (jax.nn.silu(gate) * up).astype(BF16)
    hidden = gather(hidden, "chip").reshape(rows, units)
    down = dot(hidden, wd_own) + swap(dot(hidden, wd_other).astype(BF16)).astype(F32)
    down = exchange(down.astype(BF16).reshape(n_tensor, own_rows, width), "tensor")
    mixed = (resid + jnp.sum(down.astype(F32), axis=0)).astype(BF16)
    return jnp.transpose(mixed.reshape(reqs // n_tensor, steps, width), (1, 0, 2))


def solution(mesh):
    n_batch, n_tensor = mesh.devices.shape
    pairs = Mesh(mesh.devices.reshape(n_batch // 2, 2, n_tensor), ("chip", "core", "tensor"))
    batch = ("chip", "core")
    mapped = jax.shard_map(
        per_device,
        mesh=pairs,
        in_specs=(
            P(None, None, batch),
            P(batch),
            P(batch, "tensor"),
            P(),
            P(batch, "tensor", None, None),
            P(batch, "tensor", None, None),
            P("tensor", batch),
            P(batch),
            P(batch, "tensor"),
            P(batch, "tensor"),
            P("tensor", batch),
            P(batch, None),
        ),
        out_specs=P(None, "tensor", batch),
        check_vma=False,
    )

    def run(*args):
        return mapped(*args[:12])

    return run
```
